32 devices in a mesh: group: 1, node: 2 (over core), expert: 16 (over z, y, x).
Axes of the slice: x: 2, y: 2, z: 4, core: 2. Of those that a mesh axis runs over, the one named last changes fastest.
Arguments:
- tokens: bfloat16 [512, 7168], P(('group', 'node', 'expert')), may hold values from -6 to 6
- copy_ids: int32 [512, 4], P(('group', 'node', 'expert')), may hold values from 0 to 7, all different within a row; in each aligned block of 16 rows (0 to 15, 16 to 31, ...) at most 16 rows name the same one
- route_weight: float32 [512, 4], P(('group', 'node', 'expert')), may hold values from 0.05 to 1
- placement: int32 [8], replicated, may hold values from 0 to 7, each once
- gate_up: bfloat16 [32, 7168, 512], P(('node', 'expert')), may hold values from -0.0625 to 0.0625
- down_proj: bfloat16 [32, 256, 7168], P(('node', 'expert')), may hold values from -0.1875 to 0.1875
Outputs:
- mixed: bfloat16 [512, 7168], P(('group', 'node', 'expert'))
The draws below stay inside these ranges and needn't reach their ends.
Inputs may be any that keep to these rules, and one draw needn't show every extreme that they name: `copy_ids`: each token names 4 different copies; among the 16 tokens of one device (aligned blocks of rows) no copy is named more than 16 times, a bound that some block reaches. `placement`: a permutation of the slots.
All inputs are finite; a program needn't handle non-finite values.
Results may differ from the reference program's by a relative error of at most 0.0057.
Values may be sent and summed in bfloat16 or wider, within the bound.
A program may use at most 128 MiB of HBM per device.

```python
import math
import jax
import jax.numpy as jnp
import numpy as np
from jax import lax

D = 7168
FF_DEV = 256
SHARDS = 4
TOP = 4
TOK_DEV = 16
FFW = 1024
PIECES = 32
SLOTS = 8
MOST = 16
TOKENS = 512


def levels(rng, extent, split, least, high):
    def one(axis_at, shards_of):
        heights = jax.random.uniform(jax.random.fold_in(jax.random.fold_in(rng, 6), axis_at), (shards_of,), jnp.float32, least / len(split), high / len(split))
        return jnp.repeat(jnp.exp(heights), extent[axis_at] // shards_of).reshape((-1,) + (1,) * (len(extent) - axis_at - 1))

    loudness = one(*split[0])
    for cut in split[1:]:
        loudness = loudness * one(*cut)
    return loudness


def deal_out(rng, own, number, rows, amount, top, limit, skew):
    order = jax.random.permutation(rng, amount)
    packed, common = shares(amount, rows * top, limit, skew, True), shares(amount, rows * top, limit, skew, False)
    places = jnp.arange(amount)

    def named(tallies, rotation):
        used = int((tallies > 0).sum())
        fixed = max(1, used // 4)
        passed = fixed + (places - fixed + rotation * (used - fixed)) % max(1, amount - fixed)
        return jnp.zeros((amount,), jnp.int32).at[order[jnp.where(places < fixed, places, passed)]].set(jnp.asarray(tallies, jnp.int32))

    tallies = jnp.where(number % 4 == 0, named(packed, number // 4), named(common, number - number // 4 - 1))
    mixed = jax.random.permutation(jax.random.fold_in(own, 3), amount)
    donor, sink = mixed[0:amount // 2 * 2:2], mixed[1:amount // 2 * 2:2]
    room = jnp.minimum(tallies[donor] - 1, limit - tallies[sink]) // 2
    room = jnp.where((donor == order[0]) | (sink == order[0]) | (tallies[sink] == 0), 0, jnp.maximum(room, 0))
    passed = jax.random.randint(jax.random.fold_in(own, 4), (amount // 2,), 0, 1 << 20) % (room + 1)
    tallies = tallies.at[donor].add(-passed).at[sink].add(passed)
    items = jnp.searchsorted(jnp.cumsum(tallies), jnp.arange(rows * top), side="right").astype(jnp.int32)
    listing = items.reshape(top, rows).T
    listing = listing[jax.random.permutation(jax.random.fold_in(own, 1), rows)]
    rotation = jax.random.randint(jax.random.fold_in(own, 2), (rows, 1), 0, top)
    return jnp.take_along_axis(listing, (jnp.arange(top)[None, :] + rotation) % top, axis=1)


def shares(number_of, total, reach, lean, full):
    weights = [(1 << 20) // math.isqrt(grade ** lean) + 1 for grade in range(1, number_of + 1)]
    largest = reach if full else min(reach, max(-(-total // number_of), total * weights[0] // sum(weights)))
    least = 1 if total - largest >= number_of - 1 else 0
    counts, spare = [largest] + [least] * (number_of - 1), total - largest - least * (number_of - 1)
    while spare > 0:
        movable = [i for i in range(1, number_of) if counts[i] < largest] or [i for i in range(1, number_of) if counts[i] < reach]
        whole, left = sum([weights[i] for i in movable]), spare
        for i in movable:
            more = min(reach - counts[i], max(1, left * weights[i] // whole), spare)
            counts[i] = counts[i] + more
            spare = spare - more
    return np.array(counts)


def bell_draw(key, dims, spread, most, split=(), kind=jnp.bfloat16):
    values = jax.random.normal(key, dims, jnp.float32) * spread
    if len(split) > 0:
        values = levels(key, dims, split, -0.22, 0.18) * values
    return jnp.clip(values, min=-most, max=most).astype(kind)


def setup_inputs(seed: int = 0, part: int = 0) -> dict:
    key_list = jax.random.split(jax.random.key(seed), 7)
    part_keys = jax.random.split(jax.random.fold_in(key_list[6], part), 7)
    tokens = bell_draw(part_keys[0], (TOKENS, D), 1.0, 6.0, ((0, 32),))
    copy_ids_keys = jax.random.split(jax.random.fold_in(part_keys[1], 1), TOKENS // TOK_DEV)
    copy_ids_turns = jax.random.permutation(jax.random.fold_in(part_keys[1], 3), TOKENS // TOK_DEV)
    copy_ids = jax.vmap(lambda own, number: deal_out(jax.random.fold_in(part_keys[1], 2), own, number, TOK_DEV, SLOTS, TOP, MOST, 2))(copy_ids_keys, copy_ids_turns).reshape((TOKENS, TOP))
    route_weight = jnp.clip(jnp.exp(math.log(1.0) - 2.9957323 * jax.random.uniform(part_keys[2], (TOKENS, TOP), jnp.float32) ** levels(part_keys[2], (TOKENS, TOP), ((0, 32),), -0.2, 0.2)), 0.05, 1.0)
    placement = jax.random.permutation(key_list[3], SLOTS).astype(jnp.int32)
    gate_up = bell_draw(key_list[4], (PIECES, D, 2 * FF_DEV), D ** -0.5, 0.0625, ((0, 32),))
    down_proj = bell_draw(key_list[5], (PIECES, FF_DEV, D), FFW ** -0.5, 0.1875, ((0, 32),))
    return dict(tokens=tokens, copy_ids=copy_ids, route_weight=route_weight, placement=placement, gate_up=gate_up, down_proj=down_proj)


def reference(tokens, copy_ids, route_weight, placement, gate_up, down_proj):
    tok_count = copy_ids.shape[0]
    pair_count = tok_count * TOP
    pair_index = jnp.arange(pair_count, dtype=jnp.int32)
    pair_slot = placement[copy_ids.reshape(-1)].astype(jnp.int32)
    pair_token = (pair_index // TOP).astype(jnp.int32)
    pair_weight = route_weight.reshape(-1)
    ordering = jnp.argsort(pair_slot * pair_count + pair_index).astype(jnp.int32)
    slot_range = jnp.arange(SLOTS, dtype=jnp.int32)
    slot_counts = jnp.sum((pair_slot[None, :] == slot_range[:, None]).astype(jnp.int32), axis=1).astype(jnp.int32)
    slot_starts = (jnp.cumsum(slot_counts) - slot_counts).astype(jnp.int32)
    capacity = MOST * (tok_count // TOK_DEV)
    padded = jnp.concatenate([ordering, jnp.zeros((capacity,), jnp.int32)])
    local_range = jnp.arange(capacity, dtype=jnp.int32)

    def one_piece(mixed_sum, piece_number):
        slot_number = (piece_number // SHARDS).astype(jnp.int32)
        chosen = lax.dynamic_slice_in_dim(padded, slot_starts[slot_number], capacity)
        is_valid = local_range < slot_counts[slot_number]
        owners = pair_token[chosen]
        inputs = tokens[owners]
        projected = jnp.dot(inputs, gate_up[piece_number], preferred_element_type=jnp.float32)
        hidden = (jax.nn.silu(projected[:, :FF_DEV]) * projected[:, FF_DEV:]).astype(jnp.bfloat16)
        partial_out = jnp.dot(hidden, down_proj[piece_number], preferred_element_type=jnp.float32).astype(jnp.bfloat16)
        factor = jnp.where(is_valid, pair_weight[chosen], jnp.zeros((), pair_weight.dtype))
        return mixed_sum.at[owners].add(factor[:, None] * partial_out.astype(jnp.float32)), None

    initial = jnp.zeros((tok_count, tokens.shape[1]), jnp.float32)
    mixed_sum, unused = lax.scan(one_piece, initial, jnp.arange(PIECES, dtype=jnp.int32))
    return mixed_sum.astype(jnp.bfloat16)
```

```python
import functools

import jax
import jax.numpy as jnp
from jax import lax
from jax.experimental import pallas as pl
from jax.experimental.pallas import tpu as pltpu
from jax.sharding import PartitionSpec as P

MESH = pl.DeviceIdType.MESH
PARTS = 2
LANES = 128


def layer_kernel(
    grid_dims, slots,
    placement_ref, tok_ref, ids_ref, rw_ref, gu_hbm, dn_hbm, out_ref,
    gath, gu, dn, acc, part_sum, sib_in, b_in, z_in, a_in,
    w_sem, g_recv, g_send, g_asend, s_send, s_recv, b_send, b_recv, z_send, z_recv, a_send, a_recv,
):
    depth, height, breadth = grid_dims
    chips = depth * height * breadth
    plane = height * breadth
    rows, width = tok_ref.shape
    half = width // PARTS
    hidden_units = dn.shape[0]
    top = ids_ref.shape[1]
    core = lax.axis_index("node")
    chip = lax.axis_index("expert")
    z = chip // plane
    y = (chip // breadth) % height
    x = chip % breadth
    base = core * chips
    own = base + chip
    other_base = (1 - core) * chips
    slot = own // (2 * chips // slots)

    a_dims = (breadth, height)
    b_dims = (height, breadth)
    a_pos = (x, y)
    b_pos = (y, x)

    def chip_at(p, zz, aa, bb):
        yy, xx = (bb, aa) if p == 0 else (aa, bb)
        return (zz * height + yy) * breadth + xx

    def dev(node, expert):
        return {"node": node, "expert": expert}

    sibling = dev(1 - core, chip)
    up = dev(core, chip + plane)
    down = dev(core, chip - plane)
    a_dev = tuple(dev(core, chip_at(p, z, 1 - a_pos[p], b_pos[p])) for p in range(PARTS))
    b_dev = tuple(dev(core, chip_at(p, z, a_pos[p], 1 - b_pos[p])) for p in range(PARTS))
    has_up = z < depth - 1
    has_down = z > 0

    gu_copy = pltpu.make_async_copy(gu_hbm.at[0], gu, w_sem.at[0])
    dn_copy = pltpu.make_async_copy(dn_hbm.at[0], dn, w_sem.at[1])
    gu_copy.start()
    dn_copy.start()

    barrier = pltpu.get_barrier_semaphore()
    pl.semaphore_signal(barrier, inc=1, device_id=sibling, device_id_type=MESH)
    fixed = 1
    for p in range(PARTS):
        if a_dims[p] > 1:
            pl.semaphore_signal(barrier, inc=1, device_id=a_dev[p], device_id_type=MESH)
            fixed += 1

    @pl.when(has_up)
    def _():
        pl.semaphore_signal(barrier, inc=1, device_id=up, device_id_type=MESH)

    @pl.when(has_down)
    def _():
        pl.semaphore_signal(barrier, inc=1, device_id=down, device_id_type=MESH)

    lane = lax.broadcasted_iota(jnp.int32, (rows, LANES), 1)
    weight = jnp.zeros((rows, LANES), jnp.float32)
    for s in range(slots):
        here = lane == placement_ref[s]
        for k in range(top):
            named = ids_ref[:, k : k + 1] == s
            weight = weight + jnp.where(here & named, rw_ref[:, k : k + 1], 0.0)
    coarse = weight.astype(jnp.bfloat16)
    fine = (weight - coarse.astype(jnp.float32)).astype(jnp.bfloat16)
    for p, extra in ((0, coarse), (1, fine)):
        gath[p, own, :, 0:half] = tok_ref[:, p * half : (p + 1) * half]
        gath[p, own, :, half : half + LANES] = extra

    pl.semaphore_wait(barrier, fixed + has_up.astype(jnp.int32) + has_down.astype(jnp.int32))

    def g_copy(p, kind, block, to):
        return pltpu.make_async_remote_copy(
            src_ref=gath.at[p, block], dst_ref=gath.at[p, block],
            send_sem=g_send.at[p, kind, block - base], recv_sem=g_recv.at[p, block],
            device_id=to, device_id_type=MESH)

    def g_a(p):
        return pltpu.make_async_remote_copy(
            src_ref=gath.at[p, own], dst_ref=gath.at[p, own],
            send_sem=g_asend.at[p], recv_sem=g_recv.at[p, own],
            device_id=a_dev[p], device_id_type=MESH)

    def g_wait(p, block):
        pltpu.make_async_remote_copy(
            src_ref=gath.at[p, block], dst_ref=gath.at[p, block],
            send_sem=g_asend.at[p], recv_sem=g_recv.at[p, block],
            device_id=sibling, device_id_type=MESH).wait_recv()

    def g_spread(p, block, go_up, go_down):
        if go_up is not None:
            @pl.when(go_up)
            def _():
                g_copy(p, 0, block, up).start()
        if go_down is not None:
            @pl.when(go_down)
            def _():
                g_copy(p, 1, block, down).start()
        if b_dims[p] > 1:
            g_copy(p, 2, block, b_dev[p]).start()
        g_copy(p, 3, block, sibling).start()

    for p in range(PARTS):
        if a_dims[p] > 1:
            g_a(p).start()
    for p in range(PARTS):
        g_spread(p, own, has_up, has_down)
    for p in range(PARTS):
        if a_dims[p] > 1:
            block = base + chip_at(p, z, 1 - a_pos[p], b_pos[p])
            g_wait(p, block)
            g_spread(p, block, has_up, has_down)

    def g_from_b(zz):
        for p in range(PARTS):
            if b_dims[p] > 1:
                for aa in range(a_dims[p]):
                    block = base + chip_at(p, zz, aa, 1 - b_pos[p])
                    g_wait(p, block)
                    g_copy(p, 3, block, sibling).start()

    def g_hop(h, carry):
        for low in (True, False):
            zz = z - h if low else z + h
            there = zz >= 0 if low else zz < depth

            @pl.when(there)
            def _():
                for p in range(PARTS):
                    for aa in range(a_dims[p]):
                        block = base + chip_at(p, zz, aa, b_pos[p])
                        g_wait(p, block)
                        g_spread(p, block, has_up if low else None, None if low else has_down)
        for low in (True, False):
            zz = z - (h - 1) if low else z + (h - 1)
            there = (zz >= 0) if low else ((zz < depth) & (h > 1))

            @pl.when(there)
            def _():
                g_from_b(zz)
        return carry

    lax.fori_loop(1, depth, g_hop, 0)
    for zz in (z - (depth - 1), z + (depth - 1)) if depth > 1 else (z,):
        @pl.when((zz >= 0) & (zz < depth))
        def _():
            g_from_b(zz)

    def g_other(e, carry):
        for p in range(PARTS):
            g_wait(p, other_base + e)
        return carry

    lax.fori_loop(0, chips, g_other, 0)

    gu_copy.wait()
    dn_copy.wait()
    blocks = min(chips, max(1, 256 // rows))
    per_core = chips // blocks
    tile = half // (half // 512) if half % 512 == 0 else half

    def compute(first):
        count = blocks * rows

        def rows_of(p, lo, hi):
            return gath[p, pl.ds(first, blocks), :, lo:hi].reshape(count, hi - lo)

        acc[...] = jnp.dot(rows_of(0, 0, half), gu[0:half, :], preferred_element_type=jnp.float32)
        acc[...] += jnp.dot(rows_of(1, 0, half), gu[half:width, :], preferred_element_type=jnp.float32)
        gate = acc[:, 0:hidden_units]
        hidden = (gate * jax.nn.sigmoid(gate) * acc[:, hidden_units:]).astype(jnp.bfloat16)
        both = rows_of(0, half, half + LANES).astype(jnp.float32) + rows_of(1, half, half + LANES).astype(jnp.float32)
        at = lax.broadcasted_iota(jnp.int32, (count, LANES), 1)
        factor = jnp.sum(jnp.where(at == slot, both, 0.0), axis=1, keepdims=True)
        for p in range(PARTS):
            for t in range(half // tile):
                lo = t * tile
                result = jnp.dot(hidden, dn[:, p * half + lo : p * half + lo + tile], preferred_element_type=jnp.float32)
                part_sum[p, pl.ds(first, blocks), :, lo : lo + tile] = (
                    (result * factor).astype(jnp.bfloat16).reshape(blocks, rows, tile))

    def s_copy(p, zz):
        return pltpu.make_async_remote_copy(
            src_ref=part_sum.at[p, pl.ds(other_base + zz * plane, plane)],
            dst_ref=sib_in.at[p, pl.ds(zz * plane, plane)],
            send_sem=s_send.at[p, zz], recv_sem=s_recv.at[p, zz],
            device_id=sibling, device_id_type=MESH)

    def order(i):
        return jnp.where(i % 2 == 0, depth - 1 - i // 2, i // 2)

    def compute_chunk(i, carry):
        compute(jnp.where(i < per_core, other_base, base - per_core * blocks) + i * blocks)

        @pl.when(i == per_core - 1)
        def _():
            def send(j, carry2):
                for p in range(PARTS):
                    s_copy(p, order(j)).start()
                return carry2
            lax.fori_loop(0, depth, send, 0)
        return carry

    lax.fori_loop(0, 2 * per_core, compute_chunk, 0)

    def add(p, block, incoming):
        part_sum[p, block] = (
            part_sum[p, block].astype(jnp.float32) + incoming.astype(jnp.float32)).astype(jnp.bfloat16)

    def b_copy(p, zz, aa):
        return pltpu.make_async_remote_copy(
            src_ref=part_sum.at[p, base + chip_at(p, zz, aa, 1 - b_pos[p])],
            dst_ref=b_in.at[p, zz * a_dims[p] + aa],
            send_sem=b_send.at[p, zz * a_dims[p] + aa], recv_sem=b_recv.at[p, zz * a_dims[p] + aa],
            device_id=b_dev[p], device_id_type=MESH)

    def z_copy(p, aa, zz, place, to):
        return pltpu.make_async_remote_copy(
            src_ref=part_sum.at[p, base + chip_at(p, zz, aa, b_pos[p])],
            dst_ref=z_in.at[p, place * a_dims[p] + aa],
            send_sem=z_send.at[p, zz * a_dims[p] + aa], recv_sem=z_recv.at[p, place * a_dims[p] + aa],
            device_id=to, device_id_type=MESH)

    def z_take(p, aa, zz, place):
        z_copy(p, aa, zz, place, up).wait_recv()
        add(p, base + chip_at(p, zz, aa, b_pos[p]), z_in[p, place * a_dims[p] + aa])

    def from_sibling(zz):
        for p in range(PARTS):
            s_copy(p, zz).wait_recv()
        for p in range(PARTS):
            for k in range(plane):
                add(p, base + zz * plane + k, sib_in[p, zz * plane + k])
            if b_dims[p] > 1:
                for aa in range(a_dims[p]):
                    b_copy(p, zz, aa).start()

    def along_z(zz):
        for p in range(PARTS):
            for aa in range(a_dims[p]):
                if b_dims[p] > 1:
                    b_copy(p, zz, aa).wait_recv()
                    add(p, base + chip_at(p, zz, aa, b_pos[p]), b_in[p, zz * a_dims[p] + aa])

                @pl.when(zz > z)
                def _():
                    @pl.when(has_down)
                    def _():
                        z_take(p, aa, zz, zz)
                    z_copy(p, aa, zz, zz, up).start()

                @pl.when(zz < z)
                def _():
                    @pl.when(has_up)
                    def _():
                        z_take(p, aa, zz, zz)
                    z_copy(p, aa, zz, jnp.where(zz == z - 1, depth, zz), down).start()

    def back(i, carry):
        @pl.when(i < depth)
        def _():
            from_sibling(order(i))

        @pl.when(i > 0)
        def _():
            along_z(order(i - 1))
        return carry

    lax.fori_loop(0, depth + 1, back, 0)
    for aa_off in range(2):
        for p in range(PARTS):
            if a_dims[p] > 1 or aa_off == 1:
                aa = 1 - a_pos[p] if aa_off == 0 else a_pos[p]

                @pl.when(has_down)
                def _():
                    z_take(p, aa, z, z)

                @pl.when(has_up)
                def _():
                    z_take(p, aa, z, depth)

            if a_dims[p] > 1 and aa_off == 0:
                pltpu.make_async_remote_copy(
                    src_ref=part_sum.at[p, base + chip_at(p, z, aa, b_pos[p])], dst_ref=a_in.at[p],
                    send_sem=a_send.at[p], recv_sem=a_recv.at[p],
                    device_id=a_dev[p], device_id_type=MESH).start()
    for p in range(PARTS):
        total = part_sum[p, own].astype(jnp.float32)
        if a_dims[p] > 1:
            last = pltpu.make_async_remote_copy(
                src_ref=part_sum.at[p, base + chip_at(p, z, 1 - a_pos[p], b_pos[p])], dst_ref=a_in.at[p],
                send_sem=a_send.at[p], recv_sem=a_recv.at[p],
                device_id=a_dev[p], device_id_type=MESH)
            last.wait_recv()
            total = total + a_in[p].astype(jnp.float32)
            last.wait_send()
            g_a(p).wait_send()
        out_ref[:, p * half : (p + 1) * half] = total.astype(jnp.bfloat16)

    def drain(zz, carry):
        for p in range(PARTS):
            s_copy(p, zz).wait_send()
            for aa in range(a_dims[p]):
                if b_dims[p] > 1:
                    b_copy(p, zz, aa).wait_send()
                    g_copy(p, 3, base + chip_at(p, zz, aa, 1 - b_pos[p]), sibling).wait_send()
                    g_copy(p, 2, base + chip_at(p, zz, aa, b_pos[p]), b_dev[p]).wait_send()
                block = base + chip_at(p, zz, aa, b_pos[p])
                g_copy(p, 3, block, sibling).wait_send()

                @pl.when((zz <= z) & has_up)
                def _():
                    g_copy(p, 0, block, up).wait_send()

                @pl.when((zz >= z) & has_down)
                def _():
                    g_copy(p, 1, block, down).wait_send()

                @pl.when(zz != z)
                def _():
                    z_copy(p, aa, zz, zz, up).wait_send()
        return carry

    lax.fori_loop(0, depth, drain, 0)


def shards(grid_dims, tokens, copy_ids, route_weight, placement, gate_up, down_proj):
    rows, width = tokens.shape
    slots = placement.shape[0]
    depth, height, breadth = grid_dims
    chips = depth * height * breadth
    devices = 2 * chips
    half = width // PARTS
    most = max(height, breadth)
    count = min(chips, max(1, 256 // rows)) * rows
    dma = pltpu.SemaphoreType.DMA
    vmem = pl.BlockSpec(memory_space=pltpu.VMEM)
    return pl.pallas_call(
        functools.partial(layer_kernel, grid_dims, slots),
        out_shape=jax.ShapeDtypeStruct((rows, width), jnp.bfloat16),
        in_specs=[
            pl.BlockSpec(memory_space=pltpu.SMEM), vmem, vmem, vmem,
            pl.BlockSpec(memory_space=pl.ANY), pl.BlockSpec(memory_space=pl.ANY),
        ],
        out_specs=vmem,
        scratch_shapes=[
            pltpu.VMEM((PARTS, devices, rows, half + LANES), jnp.bfloat16),
            pltpu.VMEM(gate_up.shape[1:], jnp.bfloat16),
            pltpu.VMEM(down_proj.shape[1:], jnp.bfloat16),
            pltpu.VMEM((count, gate_up.shape[2]), jnp.float32),
            pltpu.VMEM((PARTS, devices, rows, half), jnp.bfloat16),
            pltpu.VMEM((PARTS, chips, rows, half), jnp.bfloat16),
            pltpu.VMEM((PARTS, depth * most if most > 1 else 1, rows, half), jnp.bfloat16),
            pltpu.VMEM((PARTS, (depth + 1) * most, rows, half), jnp.bfloat16),
            pltpu.VMEM((PARTS, rows, half), jnp.bfloat16),
            dma((2,)),
            dma((PARTS, devices)),
            dma((PARTS, 4, chips)),
            dma((PARTS,)),
            dma((PARTS, depth)),
            dma((PARTS, depth)),
            dma((PARTS, depth * most)),
            dma((PARTS, depth * most)),
            dma((PARTS, depth * most)),
            dma((PARTS, (depth + 1) * most)),
            dma((PARTS,)),
            dma((PARTS,)),
        ],
        compiler_params=pltpu.CompilerParams(
            collective_id=0, has_side_effects=True, vmem_limit_bytes=62 * 2**20),
        cost_estimate=pl.CostEstimate(
            flops=6 * devices * rows * width * down_proj.shape[1],
            bytes_accessed=2 * 3 * width * down_proj.shape[1], transcendentals=0),
    )(placement, tokens, copy_ids, route_weight, gate_up, down_proj)


def solution(mesh):
    chips = mesh.shape["expert"]
    grid_dims = (chips // 4, 2, 2) if mesh.shape["group"] == 1 and chips % 4 == 0 else (chips, 1, 1)
    placed = (
        P(("group", "node", "expert"), None),
        P(("group", "node", "expert"), None),
        P(("group", "node", "expert"), None),
        P(),
        P(("node", "expert"), None, None),
        P(("node", "expert"), None, None),
    )
    return jax.shard_map(
        functools.partial(shards, grid_dims),
        mesh=mesh,
        in_specs=placed,
        out_specs=P(("group", "node", "expert"), None),
        check_vma=False,
    )
```

```python
import functools

import jax
import jax.numpy as jnp
from jax import lax
from jax.experimental import pallas as pl
from jax.experimental.pallas import tpu as pltpu
from jax.sharding import PartitionSpec as P

MESH = pl.DeviceIdType.MESH
PARTS = 2
LANES = 128


def layer_kernel(
    grid_dims, slots,
    placement_ref, tok_ref, ids_ref, rw_ref, gu_hbm, dn_hbm, out_ref,
    gath, gu, dn, acc, hid, fac, part_sum, sib_in, b_in, z_in, a_in, fin, f_in,
    w_sem, g_recv, g_send, gz_send, g_isend, s_send, s_recv, b_send, b_recv, z_send, z_recv,
    a_send, a_recv, f_sem,
):
    depth, side = grid_dims
    plane = side * side
    chips = depth * plane
    rows, width = tok_ref.shape
    half = width // PARTS
    hidden_units = hid.shape[1]
    top = ids_ref.shape[1]
    core = lax.axis_index("node")
    chip = lax.axis_index("expert")
    z = chip // plane
    y = (chip // side) % side
    x = chip % side
    own = core * chips + chip
    mate = (1 - core) * chips + chip
    slot = own // (2 * chips // slots)

    first = core == 0
    a_step = jnp.where(first, 1, side)
    b_step = jnp.where(first, side, 1)
    a_pos = jnp.where(first, x, y)
    b_pos = jnp.where(first, y, x)

    def chip_at(zz, aa, bb):
        return zz * plane + aa * a_step + bb * b_step

    def dev(node, expert):
        return {"node": node, "expert": expert}

    sibling = dev(1 - core, chip)
    a_dev = dev(core, chip_at(z, 1 - a_pos, b_pos))
    b_dev = dev(core, chip_at(z, a_pos, 1 - b_pos))

    w_copies = [pltpu.make_async_copy(gu_hbm.at[0], gu, w_sem.at[0])] + [
        pltpu.make_async_copy(dn_hbm.at[0, :, pl.ds(p * half, half)], dn.at[p], w_sem.at[1 + p])
        for p in range(PARTS)]
    for copy in w_copies:
        copy.start()

    barrier = pltpu.get_barrier_semaphore()
    near = [sibling] + ([a_dev, b_dev] if side > 1 else [])
    for to in near:
        pl.semaphore_signal(barrier, inc=1, device_id=to, device_id_type=MESH)

    def greet(h, carry):
        zz = lax.rem(z + h, depth)
        pl.semaphore_signal(barrier, inc=1, device_id=dev(core, chip_at(zz, a_pos, b_pos)), device_id_type=MESH)
        return carry

    lax.fori_loop(1, depth, greet, 0)

    lane = lax.broadcasted_iota(jnp.int32, (rows, LANES), 1)
    weight = jnp.zeros((rows, LANES), jnp.float32)
    for s in range(slots):
        here = lane == placement_ref[s]
        for k in range(top):
            named = ids_ref[:, k : k + 1] == s
            weight = weight + jnp.where(here & named, rw_ref[:, k : k + 1], 0.0)
    coarse = weight.astype(jnp.bfloat16)
    fine = (weight - coarse.astype(jnp.float32)).astype(jnp.bfloat16)
    for p, extra in ((0, coarse), (1, fine)):
        gath[p, own, :, 0:half] = tok_ref[:, p * half : (p + 1) * half]
        gath[p, own, :, half : half + LANES] = extra

    pl.semaphore_wait(barrier, len(near) + depth - 1)

    def remote(src, dst, send, recv, to):
        return pltpu.make_async_remote_copy(
            src_ref=src, dst_ref=dst, send_sem=send, recv_sem=recv, device_id=to, device_id_type=MESH)

    def g_copy(sem, k, ch, to):
        block = k * chips + ch
        return remote(gath.at[core, block], gath.at[core, block], sem, g_recv.at[core, block], to)

    def g_z(k, zz):
        return g_copy(gz_send.at[k, zz], k, chip, dev(core, chip_at(zz, a_pos, b_pos)))

    def g_to(kind, k, ch):
        return g_copy(g_send.at[kind, k * chips + ch], k, ch, (a_dev, b_dev, sibling)[kind])

    def g_mate(p):
        return remote(gath.at[p, own], gath.at[p, own], g_isend.at[p], g_recv.at[p, own], sibling)

    def g_wait(p, block):
        remote(gath.at[p, block], gath.at[p, block], g_isend.at[p], g_recv.at[p, block], sibling).wait_recv()

    def planes(h, act):
        @pl.when(z - h >= 0)
        def _():
            act(z - h)

        @pl.when((z + h < depth) & (h != 0))
        def _():
            act(z + h)

    def g_begin(k):
        @pl.when(core != k)
        def _():
            g_wait(core, mate)

        def one(h, carry):
            planes(h, lambda zz: g_z(k, zz).start())
            return carry

        if side > 1:
            g_to(1, k, chip).start()
            g_to(0, k, chip).start()
        lax.fori_loop(1, depth, one, 0)

    def g_steps(k, lo, hi):
        def from_z(zz):
            ch = chip_at(zz, a_pos, b_pos)
            g_wait(core, k * chips + ch)
            if side > 1:
                g_to(0, k, ch).start()
                g_to(1, k, ch).start()
            g_to(2, k, ch).start()

        def from_a(zz):
            ch = chip_at(zz, 1 - a_pos, b_pos)
            g_wait(core, k * chips + ch)
            g_to(1, k, ch).start()
            g_to(2, k, ch).start()

        def from_b(zz):
            for aa in range(side):
                ch = chip_at(zz, aa, 1 - b_pos)
                g_wait(core, k * chips + ch)
                g_to(2, k, ch).start()

        def one(h, carry):
            @pl.when((h >= 1) & (h < depth))
            def _():
                planes(h, from_z)
            if side > 1:
                @pl.when((h >= 1) & (h <= depth))
                def _():
                    planes(h - 1, from_a)

                @pl.when(h >= 2)
                def _():
                    planes(h - 2, from_b)
            return carry

        lax.fori_loop(lo, hi, one, 0)

    def g_end(k):
        def g_other(e, carry):
            @pl.when((e != chip) | (core != k))
            def _():
                g_wait(1 - core, k * chips + e)
            return carry

        lax.fori_loop(0, chips, g_other, 0)

    blocks = min(chips, max(1, 256 // rows))
    count = blocks * rows
    tile = 512 if half % 512 == 0 else half

    def gate_up(k):
        def one(i, carry):
            at = k * chips + i * blocks
            here = pl.ds(pl.multiple_of(i * count, count), count)

            def rows_of(p, lo, hi):
                return gath[p, pl.ds(at, blocks), :, lo:hi].reshape(count, hi - lo)

            acc[...] = jnp.dot(rows_of(0, 0, half), gu[0:half, :], preferred_element_type=jnp.float32)
            acc[...] += jnp.dot(rows_of(1, 0, half), gu[half:width, :], preferred_element_type=jnp.float32)
            gate = acc[:, 0:hidden_units]
            hid[here, :] = (gate * jax.nn.sigmoid(gate) * acc[:, hidden_units:]).astype(jnp.bfloat16)
            both = rows_of(0, half, half + LANES).astype(jnp.float32) + rows_of(1, half, half + LANES).astype(jnp.float32)
            lanes = lax.broadcasted_iota(jnp.int32, (count, LANES), 1)
            factor = jnp.sum(jnp.where(lanes == slot, both, 0.0), axis=1, keepdims=True)
            fac[here, :] = jnp.broadcast_to(factor, (count, LANES))
            return carry

        lax.fori_loop(0, chips // blocks, one, 0)

    def down_proj(k, p):
        def one(i, carry):
            at = k * chips + i * blocks
            here = pl.ds(pl.multiple_of(i * count, count), count)
            hidden = hid[here, :]
            factor = fac[here, 0:1]
            for t in range(half // tile):
                lo = t * tile
                result = jnp.dot(hidden, dn[p, :, lo : lo + tile], preferred_element_type=jnp.float32)
                part_sum[p, pl.ds(at, blocks), :, lo : lo + tile] = (
                    (result * factor).astype(jnp.bfloat16).reshape(blocks, rows, tile))
            return carry

        lax.fori_loop(0, chips // blocks, one, 0)

    def order(i):
        return jnp.where(i % 2 == 0, depth - 1 - i // 2, i // 2)

    def s_copy(k, zz):
        here = pl.ds(k * chips + zz * plane, plane)
        return remote(part_sum.at[1 - core, here], sib_in.at[here], s_send.at[k, zz], s_recv.at[k, zz], sibling)

    def to_sibling(k):
        def one(i, carry):
            s_copy(k, order(i)).start()
            return carry
        lax.fori_loop(0, depth, one, 0)

    def add(block, incoming):
        part_sum[core, block] = (
            part_sum[core, block].astype(jnp.float32) + incoming.astype(jnp.float32)).astype(jnp.bfloat16)

    def a_copy(k, zz):
        return remote(part_sum.at[core, k * chips + chip_at(zz, 1 - a_pos, b_pos)], a_in.at[k, zz],
                      a_send.at[k, zz], a_recv.at[k, zz], a_dev)

    def b_copy(k, zz, near_a):
        aa = a_pos if near_a else 1 - a_pos
        place = 2 * zz + (1 if near_a else 0)
        return remote(part_sum.at[core, k * chips + chip_at(zz, aa, 1 - b_pos)], b_in.at[k, place],
                      b_send.at[k, place], b_recv.at[k, place], b_dev)

    def z_copy(k, zz):
        return remote(part_sum.at[core, k * chips + chip_at(zz, a_pos, b_pos)], z_in.at[k, z],
                      z_send.at[k, zz], z_recv.at[k, z], dev(core, chip_at(zz, a_pos, b_pos)))

    def z_wait(k, zz):
        remote(z_in.at[k, zz], z_in.at[k, zz], z_send.at[k, zz], z_recv.at[k, zz], sibling).wait_recv()

    def from_sibling(k):
        def one(i, carry):
            zz = order(i)
            s_copy(k, zz).wait_recv()
            for j in range(plane):
                block = k * chips + zz * plane + j
                add(block, sib_in[block])
            if side > 1:
                b_copy(k, zz, False).start()
                b_copy(k, zz, True).start()
            return carry
        lax.fori_loop(0, depth, one, 0)

    def along_b(k, lo, hi):
        def one(i, carry):
            zz = order(i)
            for near_a in (False, True):
                b_copy(k, zz, near_a).wait_recv()
                aa = a_pos if near_a else 1 - a_pos
                add(k * chips + chip_at(zz, aa, b_pos), b_in[k, 2 * zz + (1 if near_a else 0)])
                if not near_a:
                    a_copy(k, zz).start()
            return carry
        if side > 1:
            lax.fori_loop(lo, hi, one, 0)

    def along_a(k, lo, hi):
        def one(i, carry):
            zz = order(i)
            if side > 1:
                a_copy(k, zz).wait_recv()
                add(k * chips + chip_at(zz, a_pos, b_pos), a_in[k, zz])

            @pl.when(zz != z)
            def _():
                z_copy(k, zz).start()
            return carry
        lax.fori_loop(lo, hi, one, 0)

    def along_both(k):
        def one(i, carry):
            @pl.when(i < depth)
            def _():
                along_b(k, i, i + 1)

            @pl.when(i > 0)
            def _():
                along_a(k, i - 1, i)
            return carry
        lax.fori_loop(0, depth + 1, one, 0)

    def f_copy():
        return remote(fin.at[1 - core], f_in, f_sem.at[0], f_sem.at[1], sibling)

    def finish(k):
        def one(h, total):
            def take(zz, total):
                z_wait(k, zz)
                return total + z_in[k, zz].astype(jnp.float32)
            zz = lax.rem(z + h, depth)
            return take(zz, total)
        total = lax.fori_loop(1, depth, one, part_sum[core, k * chips + chip].astype(jnp.float32))
        fin[k] = total.astype(jnp.bfloat16)

        @pl.when(core != k)
        def _():
            f_copy().start()

    for p in range(PARTS):
        g_mate(p).start()
    g_begin(0)
    g_steps(0, 1, 2)
    g_begin(1)
    g_steps(0, 2, depth + 2)
    g_steps(1, 1, 3)
    g_end(0)
    for copy in w_copies:
        copy.wait()
    gate_up(0)
    g_steps(1, 3, depth + 1)
    down_proj(0, 1 - core)
    to_sibling(0)
    down_proj(0, core)
    g_steps(1, depth + 1, depth + 2)
    from_sibling(0)
    g_end(1)
    gate_up(1)
    down_proj(1, 1 - core)
    to_sibling(1)
    along_both(0)
    down_proj(1, core)
    from_sibling(1)
    along_both(1)
    finish(0)
    finish(1)
    f_copy().wait_recv()
    for c in range(PARTS):
        @pl.when(core == c)
        def _():
            out_ref[:, c * half : (c + 1) * half] = fin[c]
            out_ref[:, (1 - c) * half : (2 - c) * half] = f_in[...]

    f_copy().wait_send()
    for p in range(PARTS):
        g_mate(p).wait_send()
    for k in range(2):
        def drain(zz, carry):
            s_copy(k, zz).wait_send()
            ch = chip_at(zz, a_pos, b_pos)
            if side > 1:
                a_copy(k, zz).wait_send()
                g_to(0, k, ch).wait_send()
                for aa in range(side):
                    b_copy(k, zz, aa == 1).wait_send()
                    g_to(1, k, chip_at(zz, aa, b_pos)).wait_send()
                    g_to(2, k, chip_at(zz, aa, 1 - b_pos)).wait_send()
                g_to(2, k, chip_at(zz, 1 - a_pos, b_pos)).wait_send()

            @pl.when(zz != z)
            def _():
                g_to(2, k, ch).wait_send()
                g_z(k, zz).wait_send()
                z_copy(k, zz).wait_send()
            return carry

        lax.fori_loop(0, depth, drain, 0)


def shards(grid_dims, tokens, copy_ids, route_weight, placement, gate_up, down_proj):
    rows, width = tokens.shape
    slots = placement.shape[0]
    depth, side = grid_dims
    chips = depth * side * side
    devices = 2 * chips
    half = width // PARTS
    hidden_units = down_proj.shape[1]
    count = min(chips, max(1, 256 // rows)) * rows
    dma = pltpu.SemaphoreType.DMA
    vmem = pl.BlockSpec(memory_space=pltpu.VMEM)
    return pl.pallas_call(
        functools.partial(layer_kernel, grid_dims, slots),
        out_shape=jax.ShapeDtypeStruct((rows, width), jnp.bfloat16),
        in_specs=[
            pl.BlockSpec(memory_space=pltpu.SMEM), vmem, vmem, vmem,
            pl.BlockSpec(memory_space=pl.ANY), pl.BlockSpec(memory_space=pl.ANY),
        ],
        out_specs=vmem,
        scratch_shapes=[
            pltpu.VMEM((PARTS, devices, rows, half + LANES), jnp.bfloat16),
            pltpu.VMEM(gate_up.shape[1:], jnp.bfloat16),
            pltpu.VMEM((PARTS, hidden_units, half), jnp.bfloat16),
            pltpu.VMEM((count, gate_up.shape[2]), jnp.float32),
            pltpu.VMEM((chips * rows, hidden_units), jnp.bfloat16),
            pltpu.VMEM((chips * rows, LANES), jnp.float32),
            pltpu.VMEM((PARTS, devices, rows, half), jnp.bfloat16),
            pltpu.VMEM((devices, rows, half), jnp.bfloat16),
            pltpu.VMEM((2, 2 * depth if side > 1 else 1, rows, half), jnp.bfloat16),
            pltpu.VMEM((2, depth, rows, half), jnp.bfloat16),
            pltpu.VMEM((2, depth if side > 1 else 1, rows, half), jnp.bfloat16),
            pltpu.VMEM((2, rows, half), jnp.bfloat16),
            pltpu.VMEM((rows, half), jnp.bfloat16),
            dma((1 + PARTS,)),
            dma((PARTS, devices)),
            dma((3, devices)),
            dma((2, depth)),
            dma((PARTS,)),
            dma((2, depth)),
            dma((2, depth)),
            dma((2, 2 * depth)),
            dma((2, 2 * depth)),
            dma((2, depth)),
            dma((2, depth)),
            dma((2, depth)),
            dma((2, depth)),
            dma((2,)),
        ],
        compiler_params=pltpu.CompilerParams(
            collective_id=0, has_side_effects=True, vmem_limit_bytes=62 * 2**20),
        cost_estimate=pl.CostEstimate(
            flops=6 * devices * rows * width * down_proj.shape[1],
            bytes_accessed=2 * 3 * width * down_proj.shape[1], transcendentals=0),
    )(placement, tokens, copy_ids, route_weight, gate_up, down_proj)


def solution(mesh):
    chips = mesh.shape["expert"]
    grid_dims = (chips // 4, 2) if mesh.shape["group"] == 1 and chips % 4 == 0 else (chips, 1)
    placed = (
        P(("group", "node", "expert"), None),
        P(("group", "node", "expert"), None),
        P(("group", "node", "expert"), None),
        P(),
        P(("node", "expert"), None, None),
        P(("node", "expert"), None, None),
    )
    return jax.shard_map(
        functools.partial(shards, grid_dims),
        mesh=mesh,
        in_specs=placed,
        out_specs=P(("group", "node", "expert"), None),
        check_vma=False,
    )
```

```python
import functools

import jax
import jax.numpy as jnp
from jax import lax
from jax.experimental import pallas as pl
from jax.experimental.pallas import tpu as pltpu
from jax.sharding import PartitionSpec as P

MESH = pl.DeviceIdType.MESH
PARTS = 2
LANES = 128


def layer_kernel(
    grid_dims, slots,
    placement_ref, tok_ref, ids_ref, rw_ref, gu_hbm, dn_hbm, out_ref,
    gath, gu, dn, acc, hid, fac, part_sum, sib_in, b_in, z_in, a_in, fin, f_in,
    w_sem, g_recv, g_send, gz_send, g_isend, s_send, s_recv, b_send, b_recv, z_send, z_recv,
    a_send, a_recv, f_sem,
):
    depth, side = grid_dims
    plane = side * side
    chips = depth * plane
    rows, width = tok_ref.shape
    half = width // PARTS
    hidden_units = hid.shape[1]
    top = ids_ref.shape[1]
    core = lax.axis_index("node")
    chip = lax.axis_index("expert")
    z = chip // plane
    y = (chip // side) % side
    x = chip % side
    own = core * chips + chip
    mate = (1 - core) * chips + chip
    slot = own // (2 * chips // slots)

    first = core == 0
    a_step = jnp.where(first, 1, side)
    b_step = jnp.where(first, side, 1)
    a_pos = jnp.where(first, x, y)
    b_pos = jnp.where(first, y, x)

    def chip_at(zz, aa, bb):
        return zz * plane + aa * a_step + bb * b_step

    def dev(node, expert):
        return {"node": node, "expert": expert}

    sibling = dev(1 - core, chip)
    a_dev = dev(core, chip_at(z, 1 - a_pos, b_pos))
    b_dev = dev(core, chip_at(z, a_pos, 1 - b_pos))

    w_copies = [pltpu.make_async_copy(gu_hbm.at[0], gu, w_sem.at[0])] + [
        pltpu.make_async_copy(dn_hbm.at[0, :, pl.ds(p * half, half)], dn.at[p], w_sem.at[1 + p])
        for p in range(PARTS)]
    for copy in w_copies:
        copy.start()

    barrier = pltpu.get_barrier_semaphore()
    near = [sibling] + ([a_dev, b_dev] if side > 1 else [])
    for to in near:
        pl.semaphore_signal(barrier, inc=1, device_id=to, device_id_type=MESH)

    def greet(h, carry):
        zz = lax.rem(z + h, depth)
        pl.semaphore_signal(barrier, inc=1, device_id=dev(core, chip_at(zz, a_pos, b_pos)), device_id_type=MESH)
        return carry

    lax.fori_loop(1, depth, greet, 0)

    lane = lax.broadcasted_iota(jnp.int32, (rows, LANES), 1)
    weight = jnp.zeros((rows, LANES), jnp.float32)
    for s in range(slots):
        here = lane == placement_ref[s]
        for k in range(top):
            named = ids_ref[:, k : k + 1] == s
            weight = weight + jnp.where(here & named, rw_ref[:, k : k + 1], 0.0)
    coarse = weight.astype(jnp.bfloat16)
    fine = (weight - coarse.astype(jnp.float32)).astype(jnp.bfloat16)
    for p, extra in ((0, coarse), (1, fine)):
        gath[p, own, :, 0:half] = tok_ref[:, p * half : (p + 1) * half]
        gath[p, own, :, half : half + LANES] = extra

    pl.semaphore_wait(barrier, len(near) + depth - 1)

    def remote(src, dst, send, recv, to):
        return pltpu.make_async_remote_copy(
            src_ref=src, dst_ref=dst, send_sem=send, recv_sem=recv, device_id=to, device_id_type=MESH)

    def g_copy(sem, k, ch, to):
        block = k * chips + ch
        return remote(gath.at[core, block], gath.at[core, block], sem, g_recv.at[core, block], to)

    def g_z(k, zz):
        return g_copy(gz_send.at[k, zz], k, chip, dev(core, chip_at(zz, a_pos, b_pos)))

    def g_to(kind, k, ch):
        return g_copy(g_send.at[kind, k * chips + ch], k, ch, (a_dev, b_dev, sibling)[kind])

    def g_mate(p):
        return remote(gath.at[p, own], gath.at[p, own], g_isend.at[p], g_recv.at[p, own], sibling)

    def g_wait(p, block):
        remote(gath.at[p, block], gath.at[p, block], g_isend.at[p], g_recv.at[p, block], sibling).wait_recv()

    def planes(h, act):
        @pl.when(z - h >= 0)
        def _():
            act(z - h)

        @pl.when((z + h < depth) & (h != 0))
        def _():
            act(z + h)

    def g_begin(k):
        @pl.when(core != k)
        def _():
            g_wait(core, mate)

        def one(h, carry):
            planes(h, lambda zz: g_z(k, zz).start())
            return carry

        if side > 1:
            g_to(1, k, chip).start()
            g_to(0, k, chip).start()
        lax.fori_loop(1, depth, one, 0)

    def g_steps(k, lo, hi):
        def from_z(zz):
            ch = chip_at(zz, a_pos, b_pos)
            g_wait(core, k * chips + ch)
            if side > 1:
                g_to(0, k, ch).start()
                g_to(1, k, ch).start()
            g_to(2, k, ch).start()

        def from_a(zz):
            ch = chip_at(zz, 1 - a_pos, b_pos)
            g_wait(core, k * chips + ch)
            g_to(1, k, ch).start()
            g_to(2, k, ch).start()

        def from_b(zz):
            for aa in range(side):
                ch = chip_at(zz, aa, 1 - b_pos)
                g_wait(core, k * chips + ch)
                g_to(2, k, ch).start()

        def one(h, carry):
            @pl.when((h >= 1) & (h < depth))
            def _():
                planes(h, from_z)
            if side > 1:
                @pl.when((h >= 1) & (h <= depth))
                def _():
                    planes(h - 1, from_a)

                @pl.when(h >= 2)
                def _():
                    planes(h - 2, from_b)
            return carry

        lax.fori_loop(lo, hi, one, 0)

    def g_end(k):
        def g_other(e, carry):
            @pl.when((e != chip) | (core != k))
            def _():
                g_wait(1 - core, k * chips + e)
            return carry

        lax.fori_loop(0, chips, g_other, 0)

    blocks = min(chips, max(1, 256 // rows))
    count = blocks * rows
    tile = 512 if half % 512 == 0 else half

    def gate_up(k):
        def one(i, carry):
            at = k * chips + i * blocks
            here = pl.ds(pl.multiple_of(i * count, count), count)

            def rows_of(p, lo, hi):
                return gath[p, pl.ds(at, blocks), :, lo:hi].reshape(count, hi - lo)

            acc[...] = jnp.dot(rows_of(0, 0, half), gu[0:half, :], preferred_element_type=jnp.float32)
            acc[...] += jnp.dot(rows_of(1, 0, half), gu[half:width, :], preferred_element_type=jnp.float32)
            gate = acc[:, 0:hidden_units]
            hid[here, :] = (gate * jax.nn.sigmoid(gate) * acc[:, hidden_units:]).astype(jnp.bfloat16)
            both = rows_of(0, half, half + LANES).astype(jnp.float32) + rows_of(1, half, half + LANES).astype(jnp.float32)
            lanes = lax.broadcasted_iota(jnp.int32, (count, LANES), 1)
            factor = jnp.sum(jnp.where(lanes == slot, both, 0.0), axis=1, keepdims=True)
            fac[here, :] = jnp.broadcast_to(factor, (count, LANES))
            return carry

        lax.fori_loop(0, chips // blocks, one, 0)

    def down_proj(k, p):
        def one(i, carry):
            at = k * chips + i * blocks
            here = pl.ds(pl.multiple_of(i * count, count), count)
            hidden = hid[here, :]
            factor = fac[here, 0:1]
            for t in range(half // tile):
                lo = t * tile
                result = jnp.dot(hidden, dn[p, :, lo : lo + tile], preferred_element_type=jnp.float32)
                part_sum[p, pl.ds(at, blocks), :, lo : lo + tile] = (
                    (result * factor).astype(jnp.bfloat16).reshape(blocks, rows, tile))
            return carry

        lax.fori_loop(0, chips // blocks, one, 0)

    def order(i):
        return jnp.where(i % 2 == 0, depth - 1 - i // 2, i // 2)

    def s_copy(k, zz):
        here = pl.ds(k * chips + zz * plane, plane)
        return remote(part_sum.at[1 - core, here], sib_in.at[here], s_send.at[k, zz], s_recv.at[k, zz], sibling)

    def to_sibling(k):
        def one(i, carry):
            s_copy(k, order(i)).start()
            return carry
        lax.fori_loop(0, depth, one, 0)

    def add(block, incoming):
        part_sum[core, block] = (
            part_sum[core, block].astype(jnp.float32) + incoming.astype(jnp.float32)).astype(jnp.bfloat16)

    def a_copy(k, zz):
        return remote(part_sum.at[core, k * chips + chip_at(zz, 1 - a_pos, b_pos)], a_in.at[k, zz],
                      a_send.at[k, zz], a_recv.at[k, zz], a_dev)

    def b_copy(k, zz, near_a):
        aa = a_pos if near_a else 1 - a_pos
        place = 2 * zz + (1 if near_a else 0)
        return remote(part_sum.at[core, k * chips + chip_at(zz, aa, 1 - b_pos)], b_in.at[k, place],
                      b_send.at[k, place], b_recv.at[k, place], b_dev)

    def z_copy(k, zz):
        return remote(part_sum.at[core, k * chips + chip_at(zz, a_pos, b_pos)], z_in.at[k, z],
                      z_send.at[k, zz], z_recv.at[k, z], dev(core, chip_at(zz, a_pos, b_pos)))

    def z_wait(k, zz):
        remote(z_in.at[k, zz], z_in.at[k, zz], z_send.at[k, zz], z_recv.at[k, zz], sibling).wait_recv()

    def from_sibling(k):
        def one(i, carry):
            zz = order(i)
            s_copy(k, zz).wait_recv()
            for j in range(plane):
                block = k * chips + zz * plane + j
                add(block, sib_in[block])
            if side > 1:
                b_copy(k, zz, False).start()
                b_copy(k, zz, True).start()
            return carry
        lax.fori_loop(0, depth, one, 0)

    def along_b(k, lo, hi):
        def one(i, carry):
            zz = order(i)
            for near_a in (False, True):
                b_copy(k, zz, near_a).wait_recv()
                aa = a_pos if near_a else 1 - a_pos
                add(k * chips + chip_at(zz, aa, b_pos), b_in[k, 2 * zz + (1 if near_a else 0)])
                if not near_a:
                    a_copy(k, zz).start()
            return carry
        if side > 1:
            lax.fori_loop(lo, hi, one, 0)

    def along_a(k, lo, hi):
        def one(i, carry):
            zz = order(i)
            if side > 1:
                a_copy(k, zz).wait_recv()
                add(k * chips + chip_at(zz, a_pos, b_pos), a_in[k, zz])

            @pl.when(zz != z)
            def _():
                z_copy(k, zz).start()
            return carry
        lax.fori_loop(lo, hi, one, 0)

    def along_both(k):
        def one(i, carry):
            @pl.when(i < depth)
            def _():
                along_b(k, i, i + 1)

            @pl.when(i > 0)
            def _():
                along_a(k, i - 1, i)
            return carry
        lax.fori_loop(0, depth + 1, one, 0)

    def f_copy():
        return remote(fin.at[1 - core], f_in, f_sem.at[0], f_sem.at[1], sibling)

    def finish(k):
        def one(h, total):
            def take(zz, total):
                z_wait(k, zz)
                return total + z_in[k, zz].astype(jnp.float32)
            zz = lax.rem(z + h, depth)
            return take(zz, total)
        total = lax.fori_loop(1, depth, one, part_sum[core, k * chips + chip].astype(jnp.float32))
        fin[k] = total.astype(jnp.bfloat16)

        @pl.when(core != k)
        def _():
            f_copy().start()

    for p in range(PARTS):
        g_mate(p).start()
    g_begin(0)
    g_steps(0, 1, 2)
    g_begin(1)
    g_steps(0, 2, depth + 1)
    g_steps(1, 1, 2)
    g_steps(0, depth + 1, depth + 2)
    g_steps(1, 2, 3)
    g_end(0)
    for copy in w_copies:
        copy.wait()

    gate_up(0)
    g_steps(1, 3, depth)
    down_proj(0, 1 - core)
    to_sibling(0)
    g_steps(1, depth, depth + 1)
    down_proj(0, core)
    from_sibling(0)
    g_steps(1, depth + 1, depth + 2)
    along_b(0, 0, depth // 2)
    g_end(1)
    gate_up(1)
    along_b(0, depth // 2, depth)
    down_proj(1, 1 - core)
    to_sibling(1)
    along_a(0, 0, depth)
    down_proj(1, core)
    from_sibling(1)
    along_both(1)
    finish(0)
    finish(1)
    f_copy().wait_recv()
    for c in range(PARTS):
        @pl.when(core == c)
        def _():
            out_ref[:, c * half : (c + 1) * half] = fin[c]
            out_ref[:, (1 - c) * half : (2 - c) * half] = f_in[...]

    f_copy().wait_send()
    for p in range(PARTS):
        g_mate(p).wait_send()
    for k in range(2):
        def drain(zz, carry):
            s_copy(k, zz).wait_send()
            ch = chip_at(zz, a_pos, b_pos)
            if side > 1:
                a_copy(k, zz).wait_send()
                g_to(0, k, ch).wait_send()
                for aa in range(side):
                    b_copy(k, zz, aa == 1).wait_send()
                    g_to(1, k, chip_at(zz, aa, b_pos)).wait_send()
                    g_to(2, k, chip_at(zz, aa, 1 - b_pos)).wait_send()
                g_to(2, k, chip_at(zz, 1 - a_pos, b_pos)).wait_send()

            @pl.when(zz != z)
            def _():
                g_to(2, k, ch).wait_send()
                g_z(k, zz).wait_send()
                z_copy(k, zz).wait_send()
            return carry

        lax.fori_loop(0, depth, drain, 0)


def shards(grid_dims, tokens, copy_ids, route_weight, placement, gate_up, down_proj):
    rows, width = tokens.shape
    slots = placement.shape[0]
    depth, side = grid_dims
    chips = depth * side * side
    devices = 2 * chips
    half = width // PARTS
    hidden_units = down_proj.shape[1]
    count = min(chips, max(1, 256 // rows)) * rows
    dma = pltpu.SemaphoreType.DMA
    vmem = pl.BlockSpec(memory_space=pltpu.VMEM)
    return pl.pallas_call(
        functools.partial(layer_kernel, grid_dims, slots),
        out_shape=jax.ShapeDtypeStruct((rows, width), jnp.bfloat16),
        in_specs=[
            pl.BlockSpec(memory_space=pltpu.SMEM), vmem, vmem, vmem,
            pl.BlockSpec(memory_space=pl.ANY), pl.BlockSpec(memory_space=pl.ANY),
        ],
        out_specs=vmem,
        scratch_shapes=[
            pltpu.VMEM((PARTS, devices, rows, half + LANES), jnp.bfloat16),
            pltpu.VMEM(gate_up.shape[1:], jnp.bfloat16),
            pltpu.VMEM((PARTS, hidden_units, half), jnp.bfloat16),
            pltpu.VMEM((count, gate_up.shape[2]), jnp.float32),
            pltpu.VMEM((chips * rows, hidden_units), jnp.bfloat16),
            pltpu.VMEM((chips * rows, LANES), jnp.float32),
            pltpu.VMEM((PARTS, devices, rows, half), jnp.bfloat16),
            pltpu.VMEM((devices, rows, half), jnp.bfloat16),
            pltpu.VMEM((2, 2 * depth if side > 1 else 1, rows, half), jnp.bfloat16),
            pltpu.VMEM((2, depth, rows, half), jnp.bfloat16),
            pltpu.VMEM((2, depth if side > 1 else 1, rows, half), jnp.bfloat16),
            pltpu.VMEM((2, rows, half), jnp.bfloat16),
            pltpu.VMEM((rows, half), jnp.bfloat16),
            dma((1 + PARTS,)),
            dma((PARTS, devices)),
            dma((3, devices)),
            dma((2, depth)),
            dma((PARTS,)),
            dma((2, depth)),
            dma((2, depth)),
            dma((2, 2 * depth)),
            dma((2, 2 * depth)),
            dma((2, depth)),
            dma((2, depth)),
            dma((2, depth)),
            dma((2, depth)),
            dma((2,)),
        ],
        compiler_params=pltpu.CompilerParams(
            collective_id=0, has_side_effects=True, vmem_limit_bytes=62 * 2**20),
        cost_estimate=pl.CostEstimate(
            flops=6 * devices * rows * width * down_proj.shape[1],
            bytes_accessed=2 * 3 * width * down_proj.shape[1], transcendentals=0),
    )(placement, tokens, copy_ids, route_weight, gate_up, down_proj)


def solution(mesh):
    chips = mesh.shape["expert"]
    grid_dims = (chips // 4, 2) if mesh.shape["group"] == 1 and chips % 4 == 0 else (chips, 1)
    placed = (
        P(("group", "node", "expert"), None),
        P(("group", "node", "expert"), None),
        P(("group", "node", "expert"), None),
        P(),
        P(("node", "expert"), None, None),
        P(("node", "expert"), None, None),
    )
    return jax.shard_map(
        functools.partial(shards, grid_dims),
        mesh=mesh,
        in_specs=placed,
        out_specs=P(("group", "node", "expert"), None),
        check_vma=False,
    )
```
